32 devices in a mesh: dp: 4 (over z), row: 4 (over x, core), col: 2 (over y).
Axes of the slice: x: 2, y: 2, z: 4, core: 2. Of those that a mesh axis runs over, the one named last changes fastest.
Arguments:
- tokens: bfloat16 [8192, 2048], P(('dp', 'row'), 'col'), may hold values from -6 to 6
- grad_out: bfloat16 [8192, 2048], P(('dp', 'row'), 'col'), may hold values from -6 to 6
- first_gain: float32 [2048], P('col'), may hold values from 0.1 to 1.9
- query_weight: bfloat16 [2048, 2048], P('col', 'row'), may hold values from -0.125 to 0.125
- key_weight: bfloat16 [2048, 2048], P('col', 'row'), may hold values from -0.125 to 0.125
- value_weight: bfloat16 [2048, 4096], P('col', 'row'), may hold values from -0.125 to 0.125
- swish_weight: bfloat16 [2048, 4096], P('col', 'row'), may hold values from -0.125 to 0.125
- group_gain: float32 [4096], P(('row', 'col')), may hold values from 0.1 to 1.9
- output_weight: bfloat16 [4096, 2048], P('row', 'col'), may hold values from -0.1875 to 0.1875
- second_gain: float32 [2048], P('col'), may hold values from 0.1 to 1.9
- gate_weight: bfloat16 [2048, 4096], P('col', 'row'), may hold values from -0.125 to 0.125
- up_weight: bfloat16 [2048, 4096], P('col', 'row'), may hold values from -0.125 to 0.125
- down_weight: bfloat16 [4096, 2048], P('row', 'col'), may hold values from -0.125 to 0.125
- decay_rate: float32 [8], P(('row', 'col')), may hold values from 0.00012207031 to 0.03515625
Outputs:
- block_out: bfloat16 [8192, 2048], P(('dp', 'row'), 'col')
- input_grad: float32 [8192, 2048], P(('dp', 'row'), 'col')
- first_gain_grad: float32 [2048], P('col')
- query_grad: float32 [2048, 2048], P('col', 'row')
- key_grad: float32 [2048, 2048], P('col', 'row')
- value_grad: float32 [2048, 4096], P('col', 'row')
- swish_grad: float32 [2048, 4096], P('col', 'row')
- group_gain_grad: float32 [4096], P(('row', 'col'))
- output_grad: float32 [4096, 2048], P('row', 'col')
- second_gain_grad: float32 [2048], P('col')
- gate_grad: float32 [2048, 4096], P('col', 'row')
- up_grad: float32 [2048, 4096], P('col', 'row')
- down_grad: float32 [4096, 2048], P('row', 'col')
The draws below stay inside these ranges and needn't reach their ends.
All inputs are finite; a program needn't handle non-finite values.
Results may differ from the reference program's by a relative error of at most 0.01405.
Values may be sent and summed in bfloat16 or wider, within the bound.
No kernel may reach another device: no remote copies, remote signals or barrier semaphores. Data moves between devices by JAX's collectives and lax.ppermute only.
A program may use at most 256 MiB of HBM per device.

```python
import math
import jax
import jax.numpy as jnp
from jax import lax

D = 2048
HEADS = 8
DK = 256
DV = 512
FF = 4096
LEN = 1024
TREP = 2048
TOKENS = 8192
QK = 2048
VD = 4096
N_DP = 4


def block_scale(own_key, extent, pieces, smallest, largest):
    def one(position, shards_of):
        draws = jax.random.uniform(jax.random.fold_in(jax.random.fold_in(own_key, 6), position), (shards_of,), jnp.float32, smallest / len(pieces), largest / len(pieces))
        return jnp.repeat(jnp.exp(draws), extent[position] // shards_of).reshape((-1,) + (1,) * (len(extent) - position - 1))

    gain = one(*pieces[0])
    for cut in pieces[1:]:
        gain = gain * one(*cut)
    return gain


def noise(own_key, shape, spread, bound, shards=(), kind=jnp.bfloat16):
    level = block_scale(own_key, shape, shards, -0.22, 0.18) if shards else 1.0
    entries = jax.random.normal(own_key, shape, jnp.float32) * spread * level
    return jnp.minimum(jnp.maximum(entries, -bound), bound).astype(kind)


def setup_inputs(seed: int = 0) -> dict:
    streams_of = jax.random.split(jax.random.key(seed), 15)
    tokens = noise(streams_of[0], (TOKENS, D), 1.0, 6.0, ((0, 16), (1, 2)))
    grad_out = noise(streams_of[1], (TOKENS, D), 1.0, 6.0, ((0, 16), (1, 2)))
    first_gain = jnp.clip(1.0 + 0.18 * jax.random.normal(streams_of[2], (D,), jnp.float32), 0.1, 1.9)
    query_weight = noise(streams_of[3], (D, QK), D ** -0.5, 0.125, ((0, 2), (1, 4)))
    key_weight = noise(streams_of[4], (D, QK), D ** -0.5, 0.125, ((0, 2), (1, 4)))
    value_weight = noise(streams_of[5], (D, VD), D ** -0.5, 0.125, ((0, 2), (1, 4)))
    swish_weight = noise(streams_of[6], (D, VD), D ** -0.5, 0.125, ((0, 2), (1, 4)))
    group_gain = jnp.clip(1.0 + 0.18 * jax.random.normal(streams_of[7], (VD,), jnp.float32), 0.1, 1.9)
    output_weight = noise(streams_of[8], (VD, D), (VD // 4) ** -0.5, 0.1875, ((0, 4), (1, 2)))
    second_gain = jnp.clip(1.0 + 0.18 * jax.random.normal(streams_of[9], (D,), jnp.float32), 0.1, 1.9)
    gate_weight = noise(streams_of[10], (D, FF), D ** -0.5, 0.125, ((0, 2), (1, 4)))
    up_weight = noise(streams_of[11], (D, FF), D ** -0.5, 0.125, ((0, 2), (1, 4)))
    down_weight = noise(streams_of[12], (FF, D), (FF // 2) ** -0.5, 0.125, ((0, 4), (1, 2)))
    decay_rate = jnp.clip(jnp.exp(math.log(0.03515625) - 5.6629605 * jax.random.uniform(streams_of[13], (HEADS,), jnp.float32) ** block_scale(streams_of[13], (HEADS,), ((0, 8),), -0.2, 0.2)), 0.00012207031, 0.03515625)
    return dict(tokens=tokens, grad_out=grad_out, first_gain=first_gain, query_weight=query_weight, key_weight=key_weight, value_weight=value_weight, swish_weight=swish_weight, group_gain=group_gain, output_weight=output_weight, second_gain=second_gain, gate_weight=gate_weight, up_weight=up_weight, down_weight=down_weight, decay_rate=decay_rate)


EPS = 1e-05
ROTARY_BASE = 10000.0

@jax.custom_vjp
def low(v):
    return lax.optimization_barrier(v.astype(jnp.bfloat16)).astype(jnp.float32)

@jax.custom_vjp
def low_back(v):
    return v

def low_keep(v):
    return (low(v), None)

def low_pass(kept, grad):
    return (grad,)

def back_keep(v):
    return (v, None)

def back_low(kept, grad):
    return (low(grad),)
low.defvjp(low_keep, low_pass)
low_back.defvjp(back_keep, back_low)

def exact_dot(left, right):
    return jnp.dot(left, right, precision=lax.Precision.HIGHEST)

def layer_normalize(row_block, gain_row):
    average = lax.optimization_barrier(jnp.mean(row_block, -1, keepdims=True))
    centred = row_block - average
    variance = lax.optimization_barrier(jnp.mean(centred * centred, -1, keepdims=True))
    return centred * lax.rsqrt(variance + EPS) * gain_row

def rotate(values, cosine, sine_part):
    half_width = values.shape[-1] // 2
    front_part = values[..., :half_width]
    back_part = values[..., half_width:]
    return jnp.concatenate((front_part * cosine - back_part * sine_part, front_part * sine_part + back_part * cosine), -1)

def block_forward(input_rows, weights, decay_rate):
    first_gain, query_weight, key_weight, value_weight, swish_weight, group_gain, output_weight, second_gain, gate_weight, up_weight, down_weight = weights
    row_count = input_rows.shape[0]
    first_in = low(layer_normalize(input_rows, first_gain))
    queries = low_back(exact_dot(first_in, query_weight)).reshape(row_count, HEADS, DK)
    keys_pre = low_back(exact_dot(first_in, key_weight)).reshape(row_count, HEADS, DK)
    valued = low_back(low(exact_dot(first_in, value_weight))).reshape(row_count, HEADS, DV)
    swish_in = low_back(exact_dot(first_in, swish_weight)).reshape(row_count, HEADS, DV)
    position_ids = jnp.arange(row_count, dtype=jnp.int32) % jnp.int32(LEN)
    positions = position_ids.astype(jnp.float32)
    half_width = DK // 2
    exponents = jnp.arange(half_width, dtype=jnp.int32).astype(jnp.float32) / jnp.float32(half_width)
    frequency = jnp.power(jnp.float32(ROTARY_BASE), -exponents)
    rotation = (positions[:, None] * frequency[None, :])[:, None, :]
    cosine = jnp.cos(rotation)
    sine_part = jnp.sin(rotation)
    query_rot = low(rotate(queries, cosine, sine_part))
    key_rot = low(rotate(keys_pre, cosine, sine_part))
    step_ids = jnp.arange(LEN, dtype=jnp.int32)
    distance = step_ids[:, None] - step_ids[None, :]
    lag_value = jnp.maximum(distance, 0).astype(decay_rate.dtype)
    decay_full = jnp.exp(-decay_rate[:, None, None] * lag_value[None])
    decay_mask = jnp.where(distance[None] >= 0, decay_full, jnp.zeros_like(decay_full))

    def retention_apply(segment):
        query_sequence_rows, key_sequence_rows, value_seq = segment
        score_matrix = jnp.einsum('ktw,ctw->tkc', query_sequence_rows, key_sequence_rows, precision=lax.Precision.HIGHEST)
        weighted = low(low_back(score_matrix) * decay_mask)
        return low_back(jnp.einsum('hnm,mhe->nhe', weighted, value_seq, precision=lax.Precision.HIGHEST))
    sequences = row_count // LEN
    retained = lax.map(jax.checkpoint(retention_apply), (query_rot.reshape(sequences, LEN, HEADS, DK), key_rot.reshape(sequences, LEN, HEADS, DK), valued.reshape(sequences, LEN, HEADS, DV))).reshape(row_count, HEADS, DV)
    average = lax.optimization_barrier(jnp.mean(retained, -1, keepdims=True))
    centred = retained - average
    variance = lax.optimization_barrier(jnp.mean(centred * centred, -1, keepdims=True))
    normed_o = centred * lax.rsqrt(jnp.maximum(variance, 1.0))
    gated = low(jax.nn.silu(swish_in) * normed_o * group_gain.reshape(HEADS, DV)).reshape(row_count, HEADS * DV)
    x_mid = input_rows + low_back(exact_dot(gated, output_weight))
    second_in = low(layer_normalize(x_mid, second_gain))
    gate_pre = low_back(exact_dot(second_in, gate_weight))
    up_pre = low_back(exact_dot(second_in, up_weight))
    hidden = low(jax.nn.gelu(gate_pre) * up_pre)
    return x_mid + low_back(exact_dot(hidden, down_weight))

def reference(tokens, grad_out, first_gain, query_weight, key_weight, value_weight, swish_weight, group_gain, output_weight, second_gain, gate_weight, up_weight, down_weight, decay_rate):
    weights = tuple((jnp.asarray(item, jnp.float32) for item in (first_gain, query_weight, key_weight, value_weight, swish_weight, group_gain, output_weight, second_gain, gate_weight, up_weight, down_weight)))
    rates = jnp.asarray(decay_rate, jnp.float32)
    input_groups = jnp.asarray(tokens, jnp.float32).reshape(N_DP, TREP, D)
    cotangents = jnp.asarray(grad_out, jnp.float32).reshape(N_DP, TREP, D)

    def forward_of(rows_in, *parameter_tree):
        return block_forward(rows_in, parameter_tree, rates)

    def group_step(totals, pair_item):
        input_rows, cotangent = pair_item
        block_rows, pullback = jax.vjp(forward_of, input_rows, *weights)
        gradient = pullback(cotangent.astype(block_rows.dtype))
        new_totals = tuple((total + grad_part.astype(total.dtype) for total, grad_part in zip(totals, gradient[1:])))
        return (new_totals, (block_rows, gradient[0]))
    start_totals = tuple((jnp.zeros(item.shape, item.dtype) for item in weights))
    totals, (outputs, input_grads) = lax.scan(group_step, start_totals, (input_groups, cotangents))
    return (outputs.reshape(TOKENS, D).astype(jnp.bfloat16), input_grads.reshape(TOKENS, D), totals[0], totals[1], totals[2], totals[3], totals[4], totals[5], totals[6], totals[7], totals[8], totals[9], totals[10])
```

```python
import jax
import jax.numpy as jnp
from jax import lax
from jax.sharding import PartitionSpec as P

LEN = 1024
EPS = 1e-05
ROTARY_BASE = 10000.0
BF = jnp.bfloat16
F32 = jnp.float32
RC = ("row", "col")


def grid_perm(target):
    pairs = []
    for row in range(4):
        for col in range(2):
            place = target(row // 2, row % 2, col)
            if place is not None:
                pairs.append((row * 2 + col, (place[0] * 2 + place[1]) * 2 + place[2]))
    return pairs


TO_COL = grid_perm(lambda x, k, y: (x, k, 1 - y))
TO_X = grid_perm(lambda x, k, y: (1 - x, k, y))
TO_CORE = grid_perm(lambda x, k, y: (x, 1 - k, y))
SEQ_IN = grid_perm(lambda x, k, y: (1 - x, k, y) if x == y else (x, k, 1 - y))
SEQ_OUT = grid_perm(lambda x, k, y: (x, k, 1 - y) if x == y else (1 - x, k, y))
CROSS = grid_perm(lambda x, k, y: (1 - x, k, 1 - y) if x != y else None)


def move(value, pairs):
    return lax.ppermute(value, RC, pairs)


def dot(left, right):
    return jnp.dot(left, right, preferred_element_type=F32)


def contract_rows(left, right):
    return lax.dot_general(left, right, (((0,), (0,)), ((), ())), preferred_element_type=F32)


def contract_cols(left, right):
    return lax.dot_general(left, right, (((1,), (1,)), ((), ())), preferred_element_type=F32)


def normalize(rows):
    average = jnp.mean(rows, 1, keepdims=True)
    centred = rows - average
    variance = jnp.mean(centred * centred, 1, keepdims=True)
    inverse = lax.rsqrt(variance + EPS)
    return centred * inverse, inverse


def norm_back(grad_rows, normed, inverse, gain):
    scaled = grad_rows * gain
    grad_in = inverse * (
        scaled
        - jnp.mean(scaled, 1, keepdims=True)
        - normed * jnp.mean(scaled * normed, 1, keepdims=True)
    )
    return grad_in, jnp.sum(grad_rows * normed, 0)


def rotate(values, cosine, sine):
    half = values.shape[1] // 2
    front, back = values[:, :half], values[:, half:]
    return jnp.concatenate((front * cosine - back * sine, front * sine + back * cosine), 1)


def rotate_back(values, cosine, sine):
    half = values.shape[1] // 2
    front, back = values[:, :half], values[:, half:]
    return jnp.concatenate((front * cosine + back * sine, back * cosine - front * sine), 1)


def gather_rows(own):
    from_x = move(own, TO_X)
    from_core = move(own, TO_CORE)
    from_both = move(from_x, TO_CORE)
    return jnp.concatenate((own, from_x, from_core, from_both), 0)


def scatter_rows(front, back):
    quarter = front.shape[0] // 2
    half = front + move(back.astype(BF), TO_CORE).astype(F32)
    return half[:quarter] + move(half[quarter:].astype(BF), TO_X).astype(F32)


def partner_block(block, parity):
    half = block.shape[0] // 2
    first = move(lax.dynamic_slice_in_dim(block, parity * half, half, 0), TO_COL)
    count = lax.axis_size("dp")
    second = lax.ppermute(first, "dp", [(i, i ^ 1) for i in range(count)])
    even = parity == 0
    return jnp.concatenate(
        (jnp.where(even, first, second), jnp.where(even, second, first)), 0
    )


def replica_totals(parts):
    count = lax.axis_size("dp")
    if count != 4:
        return [lax.psum(part, "dp").astype(F32) for part in parts]
    place = lax.axis_index("dp")
    outer = (place == 0) | (place == 3)
    n = len(parts)
    totals = [None] * n
    finals = []
    for step in range(n + 2):
        if step < n and step >= 2:
            sent = jnp.where(outer, parts[step], totals[step - 2])
        elif step < n:
            sent = parts[step]
        else:
            sent = totals[step - 2]
        got = lax.ppermute(sent, "dp", [(0, 1), (1, 0), (2, 3), (3, 2)])
        if step >= 2:
            finals.append(jnp.where(outer, got, totals[step - 2]).astype(F32))
        if step < n:
            local = lax.optimization_barrier(
                (parts[step].astype(F32) + got.astype(F32)).astype(BF)
            )
            other = lax.ppermute(local, "dp", [(1, 2), (2, 1)])
            totals[step] = lax.optimization_barrier(
                (local.astype(F32) + other.astype(F32)).astype(BF)
            )
    return finals


def body(
    tokens,
    grad_out,
    first_gain,
    query_weight,
    key_weight,
    value_weight,
    swish_weight,
    group_gain,
    output_weight,
    second_gain,
    gate_weight,
    up_weight,
    down_weight,
    decay_rate,
):
    row = lax.axis_index("row")
    y = lax.axis_index("col")
    place = lax.axis_index("dp")
    x, k = row // 2, row % 2
    parity = place % 2
    same = x == y
    rows_dev, width = tokens.shape
    quarter = rows_dev // 2

    def sequence_rows(block):
        got = move(block, SEQ_IN)
        cross = move(block, CROSS)
        mine = jnp.where(same, block, got)
        other = jnp.where(same, got, cross)
        both = jnp.concatenate((mine, other), 1)
        return jnp.concatenate(
            (
                lax.dynamic_slice_in_dim(both, x * quarter, quarter, 0),
                lax.dynamic_slice_in_dim(both, (1 - x) * quarter, quarter, 0),
            ),
            0,
        )

    def home(rows):
        mine, other = rows[:, :width], rows[:, width:]
        got = move(jnp.where(same, other, mine).astype(BF), SEQ_OUT)
        cross = move(other.astype(BF), CROSS)
        here = jnp.where(same, mine, got.astype(rows.dtype))
        there = jnp.where(same, got, cross).astype(rows.dtype)
        return jnp.where(
            x == 0, jnp.concatenate((here, there), 0), jnp.concatenate((there, here), 0)
        )

    head_values = group_gain.shape[0]
    small = jnp.concatenate((first_gain, second_gain, group_gain, decay_rate))
    small_other = move(small, TO_COL)
    first_gain_full = jnp.concatenate((first_gain, small_other[:width]))
    second_gain_full = jnp.concatenate((second_gain, small_other[width : 2 * width]))
    own_group = (group_gain, small_other[2 * width : 2 * width + head_values])
    own_rate = (decay_rate[0], small_other[2 * width + head_values])
    group_gains = tuple(jnp.where(y == 0, own_group[i], own_group[1 - i]) for i in range(2))
    rates = tuple(jnp.where(y == 0, own_rate[i], own_rate[1 - i]) for i in range(2))

    input_half = sequence_rows(tokens)
    weights = {}
    query_other = partner_block(query_weight, parity)
    key_other = partner_block(key_weight, parity)
    value_other = partner_block(value_weight, parity)
    swish_other = partner_block(swish_weight, parity)
    output_other = partner_block(output_weight, parity)
    gate_other = partner_block(gate_weight, parity)
    up_other = partner_block(up_weight, parity)
    down_other = partner_block(down_weight, parity)

    input_rows = input_half.astype(F32)
    half_normed, half_inv = normalize(input_rows)
    first_half = (half_normed * first_gain_full).astype(BF)
    first_in = jnp.concatenate((first_half, move(first_half, TO_CORE)), 0)
    own_input = input_rows[:quarter]
    first_normed, first_inv = half_normed[:quarter], half_inv[:quarter]
    grad_half = sequence_rows(grad_out)
    grad_rows = jnp.concatenate((grad_half, move(grad_half, TO_CORE)), 0)
    own_grad = grad_half[:quarter].astype(F32)

    def project(rows, mine, other):
        return dot(rows[:, :width], mine) + dot(rows[:, width:], other)

    queries = project(first_in, query_weight, query_other)
    keys_pre = project(first_in, key_weight, key_other)
    valued = project(first_in, value_weight, value_other).astype(BF)
    swish_in = project(first_in, swish_weight, swish_other)

    base = 2 * k + x
    block_ids = jnp.bitwise_xor(base, jnp.arange(4, dtype=jnp.int32))
    positions = (
        block_ids[:, None] * quarter + jnp.arange(quarter, dtype=jnp.int32)[None, :]
    ).reshape(-1)
    key_size = queries.shape[1] // 2
    value_size = valued.shape[1] // 2
    half_key = key_size // 2
    frequency = ROTARY_BASE ** (-jnp.arange(half_key, dtype=F32) / half_key)
    rotation = positions.astype(F32)[:, None] * frequency[None, :]
    cosine, sine = jnp.cos(rotation), jnp.sin(rotation)
    distance = positions[:, None] - positions[None, :]
    lag = jnp.maximum(distance, 0).astype(F32)

    saved = []
    gated_heads = []
    for head in range(2):
        mask = jnp.where(distance >= 0, jnp.exp(-rates[head] * lag), 0.0)
        keys = slice(head * key_size, (head + 1) * key_size)
        values = slice(head * value_size, (head + 1) * value_size)
        query_rot = rotate(queries[:, keys], cosine, sine).astype(BF)
        key_rot = rotate(keys_pre[:, keys], cosine, sine).astype(BF)
        value_low = valued[:, values]
        scores = (contract_cols(query_rot, key_rot) * mask).astype(BF)
        retained = dot(scores, value_low)
        average = jnp.mean(retained, 1, keepdims=True)
        centred = retained - average
        variance = jnp.mean(centred * centred, 1, keepdims=True)
        floor_open = (variance > 1.0).astype(F32)
        group_inv = lax.rsqrt(jnp.maximum(variance, 1.0))
        normed_o = centred * group_inv
        swish_out, swish_pull = jax.vjp(jax.nn.silu, swish_in[:, values])
        gated_heads.append((swish_out * normed_o * group_gains[head]).astype(BF))
        saved.append(
            (mask, query_rot, key_rot, value_low, scores, floor_open, group_inv, normed_o, swish_out, swish_pull)
        )
    gated = jnp.concatenate(gated_heads, 1)

    half_rows = 2 * quarter

    def project_scatter(rows, mine, other):
        back, front = rows[half_rows:], rows[:half_rows]
        back = jnp.concatenate((dot(back, mine), dot(back, other)), 1)
        front = jnp.concatenate((dot(front, mine), dot(front, other)), 1)
        return scatter_rows(front, back)

    x_mid = own_input + project_scatter(gated, output_weight, output_other)
    second_normed, second_inv = normalize(x_mid)
    second_in = gather_rows((second_normed * second_gain_full).astype(BF))
    gate_pre = project(second_in, gate_weight, gate_other)
    up_pre = project(second_in, up_weight, up_other)
    gelu_val, gelu_pull = jax.vjp(jax.nn.gelu, gate_pre)
    hidden = (gelu_val * up_pre).astype(BF)

    def split_grad(left, right):
        return contract_rows(left[:, :width], right), contract_rows(left[:, width:], right)

    def col_total(mine, other):
        return (mine + move(other.astype(BF), TO_COL).astype(F32)).astype(BF)

    def width_grad_in(left, right):
        other = contract_rows(left[:, width:], right)
        return col_total(contract_rows(left[:, :width], right), other)

    def width_grad_out(left, right):
        other = contract_rows(left, right[:, width:])
        return col_total(contract_rows(left, right[:, :width]), other)

    down_part = width_grad_out(hidden, grad_rows)
    grad_hidden = contract_cols(grad_rows[:, :width], down_weight) + contract_cols(
        grad_rows[:, width:], down_other
    )
    grad_gate = gelu_pull(grad_hidden * up_pre)[0].astype(BF)
    grad_up = (grad_hidden * gelu_val).astype(BF)

    def back_scatter(terms):
        def total(rows):
            out = []
            for side in (1, 2):
                part = None
                for term in terms:
                    value = contract_cols(term[0][rows], term[side])
                    part = value if part is None else part + value
                out.append(part)
            return jnp.concatenate(out, 1)

        return scatter_rows(total(slice(0, half_rows)), total(slice(half_rows, None)))

    grad_second = back_scatter(
        ((grad_gate, gate_weight, gate_other), (grad_up, up_weight, up_other))
    )
    gate_part = width_grad_in(second_in, grad_gate)
    up_part = width_grad_in(second_in, grad_up)
    grad_norm_mid, second_gain_part = norm_back(
        grad_second, second_normed, second_inv, second_gain_full
    )
    grad_mid = own_grad + grad_norm_mid
    block_out = home((x_mid + project_scatter(hidden, down_weight, down_other)).astype(BF))

    attn_in = gather_rows(grad_mid.astype(BF))
    grad_gated = contract_cols(attn_in[:, :width], output_weight) + contract_cols(
        attn_in[:, width:], output_other
    )
    output_part = width_grad_out(gated, attn_in)

    grad_queries, grad_keys, grad_values, grad_swishes, group_gain_parts = [], [], [], [], []
    for head in range(2):
        (mask, query_rot, key_rot, value_low, scores, floor_open, group_inv, normed_o, swish_out, swish_pull) = saved[head]
        values = slice(head * value_size, (head + 1) * value_size)
        grad_head = grad_gated[:, values]
        group_gain_parts.append(jnp.sum(grad_head * swish_out * normed_o, 0))
        product = grad_head * group_gains[head]
        grad_normed = product * swish_out
        grad_swishes.append(swish_pull(product * normed_o)[0].astype(BF))
        grad_retained = (
            group_inv
            * (
                grad_normed
                - jnp.mean(grad_normed, 1, keepdims=True)
                - floor_open * normed_o * jnp.mean(grad_normed * normed_o, 1, keepdims=True)
            )
        ).astype(BF)
        grad_values.append(contract_rows(scores, grad_retained).astype(BF))
        grad_scores = (contract_cols(grad_retained, value_low) * mask).astype(BF)
        grad_queries.append(rotate_back(dot(grad_scores, key_rot), cosine, sine).astype(BF))
        grad_keys.append(
            rotate_back(contract_rows(grad_scores, query_rot), cosine, sine).astype(BF)
        )
    grad_query = jnp.concatenate(grad_queries, 1)
    grad_key = jnp.concatenate(grad_keys, 1)
    grad_value = jnp.concatenate(grad_values, 1)
    grad_swish = jnp.concatenate(grad_swishes, 1)

    swish_part = width_grad_in(first_in, grad_swish)
    value_part = width_grad_in(first_in, grad_value)
    query_key_part = width_grad_in(first_in, jnp.concatenate((grad_query, grad_key), 1))

    down_grad, gate_grad, up_grad, output_grad, swish_grad, value_grad, query_key_grad = (
        replica_totals(
            [down_part, gate_part, up_part, output_part, swish_part, value_part, query_key_part]
        )
    )
    head_cols = query_weight.shape[1]
    query_grad, key_grad = query_key_grad[:, :head_cols], query_key_grad[:, head_cols:]

    grad_first = back_scatter(
        (
            (grad_query, query_weight, query_other),
            (grad_key, key_weight, key_other),
            (grad_value, value_weight, value_other),
            (grad_swish, swish_weight, swish_other),
        )
    )
    grad_norm_in, first_gain_part = norm_back(
        grad_first, first_normed, first_inv, first_gain_full
    )
    input_grad = home(grad_mid + grad_norm_in)

    group_pair = jnp.where(
        y == 0,
        jnp.stack(group_gain_parts),
        jnp.stack(group_gain_parts[::-1]),
    )
    outgoing = jnp.concatenate((first_gain_part[width:], second_gain_part[width:], group_pair[1]))
    incoming = move(outgoing, TO_COL)
    gains = jnp.concatenate((first_gain_part[:width], second_gain_part[:width])) + incoming[: 2 * width]
    group_own = group_pair[0] + incoming[2 * width :]
    rows = lax.axis_size("row")
    placed = jnp.where(jnp.arange(rows)[:, None] == row, group_own[None, :], 0.0).reshape(-1)
    gains = lax.psum(jnp.concatenate((gains, placed)), ("dp", "row"))
    group_gain_grad = lax.dynamic_slice_in_dim(gains[2 * width :], row * head_values, head_values)
    return (
        block_out,
        input_grad,
        gains[:width],
        query_grad,
        key_grad,
        value_grad,
        swish_grad,
        group_gain_grad,
        output_grad,
        gains[width : 2 * width],
        gate_grad,
        up_grad,
        down_grad,
    )


def solution(mesh):
    placed = (
        P(("dp", "row"), "col"),
        P(("dp", "row"), "col"),
        P("col"),
        P("col", "row"),
        P("col", "row"),
        P("col", "row"),
        P("col", "row"),
        P(("row", "col")),
        P("row", "col"),
        P("col"),
        P("col", "row"),
        P("col", "row"),
        P("row", "col"),
        P(("row", "col")),
    )
    return jax.shard_map(
        body,
        mesh=mesh,
        in_specs=placed,
        out_specs=(
            P(("dp", "row"), "col"),
            P(("dp", "row"), "col"),
            P("col"),
            P("col", "row"),
            P("col", "row"),
            P("col", "row"),
            P("col", "row"),
            P(("row", "col")),
            P("row", "col"),
            P("col"),
            P("col", "row"),
            P("col", "row"),
            P("row", "col"),
        ),
        check_vma=False,
    )
```

```python
import jax
import jax.numpy as jnp
from jax import lax
from jax.sharding import PartitionSpec as P

LEN = 1024
EPS = 1e-05
ROTARY_BASE = 10000.0
BF = jnp.bfloat16
F32 = jnp.float32
RC = ("row", "col")


def grid_perm(target):
    pairs = []
    for row in range(4):
        for col in range(2):
            place = target(row // 2, row % 2, col)
            if place is not None:
                pairs.append((row * 2 + col, (place[0] * 2 + place[1]) * 2 + place[2]))
    return pairs


TO_COL = grid_perm(lambda x, k, y: (x, k, 1 - y))
TO_X = grid_perm(lambda x, k, y: (1 - x, k, y))
TO_CORE = grid_perm(lambda x, k, y: (x, 1 - k, y))
SEQ_IN = grid_perm(lambda x, k, y: (1 - x, k, y) if x == y else (x, k, 1 - y))
SEQ_OUT = grid_perm(lambda x, k, y: (x, k, 1 - y) if x == y else (1 - x, k, y))
CROSS = grid_perm(lambda x, k, y: (1 - x, k, 1 - y) if x != y else None)


class Line:
    def __init__(self):
        self.token = lax.create_token()

    def take(self, *values):
        *held, self.token = lax.optimization_barrier(values + (self.token,))
        return held[0] if len(held) == 1 else tuple(held)

    def step(self, work, *inputs):
        held = self.take(*inputs)
        results = work(*held) if len(inputs) > 1 else work(held)
        return self.take(*results) if isinstance(results, tuple) else self.take(results)


def move(value, pairs):
    return lax.ppermute(value, RC, pairs)


def dot(left, right):
    return jnp.dot(left, right, preferred_element_type=F32)


def contract_rows(left, right):
    return lax.dot_general(left, right, (((0,), (0,)), ((), ())), preferred_element_type=F32)


def contract_cols(left, right):
    return lax.dot_general(left, right, (((1,), (1,)), ((), ())), preferred_element_type=F32)


def normalize(rows):
    average = jnp.mean(rows, 1, keepdims=True)
    centred = rows - average
    variance = jnp.mean(centred * centred, 1, keepdims=True)
    inverse = lax.rsqrt(variance + EPS)
    return centred * inverse, inverse


def norm_back(grad_rows, normed, inverse, gain):
    scaled = grad_rows * gain
    grad_in = inverse * (
        scaled
        - jnp.mean(scaled, 1, keepdims=True)
        - normed * jnp.mean(scaled * normed, 1, keepdims=True)
    )
    return grad_in, jnp.sum(grad_rows * normed, 0)


def rotate(values, cosine, sine):
    half = values.shape[1] // 2
    front, back = values[:, :half], values[:, half:]
    return jnp.concatenate((front * cosine - back * sine, front * sine + back * cosine), 1)


def rotate_back(values, cosine, sine):
    half = values.shape[1] // 2
    front, back = values[:, :half], values[:, half:]
    return jnp.concatenate((front * cosine + back * sine, back * cosine - front * sine), 1)


OUTER = [(0, 1), (1, 0), (2, 3), (3, 2)]
INNER = [(1, 2), (2, 1)]
LAG = 3


class ReplicaTotals:
    def __init__(self, line, count):
        self.line = line
        self.count = count
        self.four = lax.axis_size("dp") == 4
        place = lax.axis_index("dp")
        self.outer = (place == 0) | (place == 3)
        self.mine, self.far, self.parts, self.got = [], [], [], []
        self.local, self.other, self.totals, self.finals = [], [], [], []

    def start(self, tile, *inputs):
        far, mine = self.line.step(lambda *held: tile(*held), *inputs)
        self.far.append(move(far, TO_COL))
        self.mine.append(mine)

    def turn(self, index):
        if not self.four:
            if index < self.count:
                part = self.line.step(
                    lambda mine, far: (mine.astype(F32) + far.astype(F32)).astype(BF),
                    self.mine[index],
                    self.far[index],
                )
                self.finals.append(lax.psum(part, "dp").astype(F32))
            return
        count = self.count
        back = index - LAG
        if index < count:
            if back >= 0:
                def join(mine, far, total):
                    part = (mine.astype(F32) + far.astype(F32)).astype(BF)
                    return part, jnp.where(self.outer, part, total)

                part, sent = self.line.step(
                    join, self.mine[index], self.far[index], self.totals[back]
                )
            else:
                part = self.line.step(
                    lambda mine, far: (mine.astype(F32) + far.astype(F32)).astype(BF),
                    self.mine[index],
                    self.far[index],
                )
                sent = part
            self.parts.append(part)
            self.got.append(lax.ppermute(sent, "dp", OUTER))
        elif index < count + LAG:
            self.got.append(lax.ppermute(self.totals[back], "dp", OUTER))

        before = index - 1
        if 0 <= before < count:
            local = self.line.step(
                lambda part, got: (part.astype(F32) + got.astype(F32)).astype(BF),
                self.parts[before],
                self.got[before],
            )
            self.local.append(local)
            self.other.append(lax.ppermute(local, "dp", INNER))
        earlier = index - 2
        if 0 <= earlier < count:
            self.totals.append(
                self.line.step(
                    lambda local, other: (local.astype(F32) + other.astype(F32)).astype(BF),
                    self.local[earlier],
                    self.other[earlier],
                )
            )
        ready = before - LAG
        if 0 <= ready < count:
            self.finals.append(
                self.line.step(
                    lambda got, total: jnp.where(self.outer, got, total).astype(F32),
                    self.got[before],
                    self.totals[ready],
                )
            )


def body(
    tokens,
    grad_out,
    first_gain,
    query_weight,
    key_weight,
    value_weight,
    swish_weight,
    group_gain,
    output_weight,
    second_gain,
    gate_weight,
    up_weight,
    down_weight,
    decay_rate,
):
    row = lax.axis_index("row")
    y = lax.axis_index("col")
    place = lax.axis_index("dp")
    x, k = row // 2, row % 2
    parity = place % 2
    same = x == y
    rows_dev, width = tokens.shape
    quarter = rows_dev // 2

    def sequence_rows(block, got, cross):
        mine = jnp.where(same, block, got)
        other = jnp.where(same, got, cross)
        both = jnp.concatenate((mine, other), 1)
        return jnp.concatenate(
            (
                lax.dynamic_slice_in_dim(both, x * quarter, quarter, 0),
                lax.dynamic_slice_in_dim(both, (1 - x) * quarter, quarter, 0),
            ),
            0,
        )

    def home(rows):
        mine, other = rows[:, :width], rows[:, width:]
        got = move(jnp.where(same, other, mine).astype(BF), SEQ_OUT)
        cross = move(other.astype(BF), CROSS)
        here = jnp.where(same, mine, got.astype(rows.dtype))
        there = jnp.where(same, got, cross).astype(rows.dtype)
        return jnp.where(
            x == 0, jnp.concatenate((here, there), 0), jnp.concatenate((there, here), 0)
        )

    head_values = group_gain.shape[0]
    small = jnp.concatenate((first_gain, second_gain, group_gain, decay_rate))
    small_other = move(small, TO_COL)
    line = Line()
    step, take = line.step, line.take

    count = lax.axis_size("dp")
    even = parity == 0
    swap = [(i, i ^ 1) for i in range(count)]

    def send_half(block):
        half = block.shape[0] // 2
        return lax.dynamic_slice_in_dim(block, parity * half, half, 0)

    def join_halves(first, second):
        return jnp.concatenate(
            (jnp.where(even, first, second), jnp.where(even, second, first)), 0
        )

    def over_dp(value):
        return lax.ppermute(value, "dp", swap)

    def over_col(value):
        return move(value, TO_COL)

    base = 2 * k + x
    block_ids = jnp.bitwise_xor(base, jnp.arange(4, dtype=jnp.int32))
    positions = (
        block_ids[:, None] * quarter + jnp.arange(quarter, dtype=jnp.int32)[None, :]
    ).reshape(-1)
    key_size = query_weight.shape[1] // 2
    value_size = value_weight.shape[1] // 2
    half_key = key_size // 2
    frequency = ROTARY_BASE ** (-jnp.arange(half_key, dtype=F32) / half_key)
    rotation = positions.astype(F32)[:, None] * frequency[None, :]
    distance = positions[:, None] - positions[None, :]
    lag = jnp.maximum(distance, 0).astype(F32)
    head_cols = query_weight.shape[1]
    values = [slice(head * value_size, (head + 1) * value_size) for head in range(2)]

    token_seq, token_cross = move(tokens, SEQ_IN), move(tokens, CROSS)
    query_key_half = over_col(
        step(lambda q, w: send_half(jnp.concatenate((q, w), 1)), query_weight, key_weight)
    )
    cosine, sine = step(lambda turns: (jnp.cos(turns), jnp.sin(turns)), rotation)

    def first_norm(block, got, cross, other_small):
        gain = jnp.concatenate((first_gain, other_small[:width]))
        rows = sequence_rows(block, got, cross).astype(F32)
        normed, inverse = normalize(rows)
        return (normed * gain).astype(BF), rows[:quarter]

    value_half = over_col(step(send_half, value_weight))
    first_half, own_input = step(first_norm, tokens, token_seq, token_cross, small_other)
    first_core = move(first_half, TO_CORE)
    swish_half = over_col(step(send_half, swish_weight))
    second_gain_full = jnp.concatenate((second_gain, small_other[width : 2 * width]))
    first_gain_full = jnp.concatenate((first_gain, small_other[:width]))
    own_group = (group_gain, small_other[2 * width : 2 * width + head_values])
    own_rate = (decay_rate[0], small_other[2 * width + head_values])
    group_gains = tuple(jnp.where(y == 0, own_group[i], own_group[1 - i]) for i in range(2))
    rates = tuple(jnp.where(y == 0, own_rate[i], own_rate[1 - i]) for i in range(2))

    query_key_half = take(query_key_half)
    query_key_swap = over_dp(query_key_half)

    def mine_first(half, core):
        full = jnp.concatenate((half, core), 0)
        rows = full[:, :width]
        return (
            full,
            dot(rows, query_weight),
            dot(rows, key_weight),
            dot(rows, value_weight),
            dot(rows, swish_weight),
        )

    first_in, query_mine, key_mine, value_mine, swish_mine = step(mine_first, first_half, first_core)
    output_send = step(send_half, output_weight)
    value_half = take(value_half)
    value_swap = over_dp(value_half)
    output_half = over_col(output_send)

    masks = step(
        lambda far, near: tuple(
            jnp.where(near >= 0, jnp.exp(-rate * far), 0.0) for rate in rates
        ),
        lag,
        distance,
    )

    def other_query_key(rows, half, swapped, query, key, cos, sin):
        other = join_halves(half, swapped)
        rows = rows[:, width:]
        query = query + dot(rows, other[:, :head_cols])
        key = key + dot(rows, other[:, head_cols:])
        out = [other]
        for head in range(2):
            cut = slice(head * key_size, (head + 1) * key_size)
            out.append(rotate(query[:, cut], cos, sin).astype(BF))
            out.append(rotate(key[:, cut], cos, sin).astype(BF))
        return tuple(out)

    query_key_other, *turned = step(
        other_query_key, first_in, query_key_half, query_key_swap, query_mine, key_mine, cosine, sine
    )
    query_rot, key_rot = turned[::2], turned[1::2]
    query_other, key_other = query_key_other[:, :head_cols], query_key_other[:, head_cols:]

    scores = [
        step(
            lambda q, w, m: (contract_cols(q, w) * m).astype(BF),
            query_rot[head],
            key_rot[head],
            masks[head],
        )
        for head in range(2)
    ]
    swish_half = take(swish_half)
    swish_swap = over_dp(swish_half)

    def other_value(rows, half, swapped, value):
        other = join_halves(half, swapped)
        return other, (value + dot(rows[:, width:], other)).astype(BF)

    value_other, valued = step(other_value, first_in, value_half, value_swap, value_mine)
    grad_held = take(grad_out)
    grad_seq, grad_cross = move(grad_held, SEQ_IN), move(grad_held, CROSS)

    def retain(weighted, value):
        retained = dot(weighted, value)
        average = jnp.mean(retained, 1, keepdims=True)
        centred = retained - average
        variance = jnp.mean(centred * centred, 1, keepdims=True)
        inverse = lax.rsqrt(jnp.maximum(variance, 1.0))
        return centred * inverse, inverse, (variance > 1.0).astype(F32)

    retained = [step(retain, scores[0], valued[:, values[0]])]
    output_half = take(output_half)
    output_swap = over_dp(output_half)
    gate_half = over_col(step(send_half, gate_weight))
    retained.append(step(retain, scores[1], valued[:, values[1]]))

    def gating(rows, half, swapped, swish, first_normed, second_normed, gain0, gain1):
        other = join_halves(half, swapped)
        swish = swish + dot(rows[:, width:], other)
        gate = jax.nn.silu(swish)
        gated = jnp.concatenate(
            (
                gate[:, values[0]] * first_normed * gain0,
                gate[:, values[1]] * second_normed * gain1,
            ),
            1,
        )
        return other, swish, gated.astype(BF)

    swish_other, swish_in, gated = step(
        gating,
        first_in,
        swish_half,
        swish_swap,
        swish_mine,
        retained[0][0],
        retained[1][0],
        *group_gains,
    )
    up_half = over_col(step(send_half, up_weight))
    grad_half = step(sequence_rows, grad_out, grad_seq, grad_cross)
    grad_core = move(grad_half, TO_CORE)

    half_rows = 2 * quarter

    def project(rows, mine, other):
        return dot(rows, mine), dot(rows, other)

    def project_scatter(rows, mine, other):
        back = step(
            lambda r, m, o: jnp.concatenate(
                (dot(r, m).astype(BF), dot(r, o).astype(BF)), 1
            ),
            rows[half_rows:],
            mine,
            other,
        )
        from_core = move(back, TO_CORE)
        front = step(
            lambda r, m, o: jnp.concatenate((dot(r, m), dot(r, o)), 1), rows[:half_rows], mine, other
        )
        return reduce_row(front, from_core)

    def reduce_row(front, from_core):
        def add(part, core):
            both = part + core.astype(F32)
            return both[:quarter], both[quarter:].astype(BF)

        own, away = step(add, front, from_core)
        return own, move(away, TO_X)

    output_other = step(join_halves, output_half, output_swap)
    gate_half = take(gate_half)
    gate_swap = over_dp(gate_half)
    own_out, out_x = project_scatter(gated, output_weight, output_other)
    grad_rows = step(lambda a, b: jnp.concatenate((a, b), 0), grad_half, grad_core)
    down_half = over_col(step(send_half, down_weight))

    def second_norm(rows, own, away, gain):
        mid = rows + own + away.astype(F32)
        normed, inverse = normalize(mid)
        return mid, normed, inverse, (normed * gain).astype(BF)

    x_mid, second_normed, second_inv, second_own = step(
        second_norm, own_input, own_out, out_x, second_gain_full
    )

    def gather_start(own):
        return move(own, TO_X), move(own, TO_CORE)

    second_x, second_core = gather_start(second_own)
    up_half = take(up_half)
    up_swap = over_dp(up_half)
    gate_other = step(join_halves, gate_half, gate_swap)
    second_x = take(second_x)
    second_both = move(second_x, TO_CORE)
    up_other = step(join_halves, up_half, up_swap)
    down_half = take(down_half)
    down_swap = over_dp(down_half)

    def feed(own, from_x, core, both, gate_o, up_o):
        rows = jnp.concatenate((own, from_x, core, both), 0)
        near, far = rows[:, :width], rows[:, width:]
        gate_pre = dot(near, gate_weight) + dot(far, gate_o)
        up_pre = dot(near, up_weight) + dot(far, up_o)
        return rows, gate_pre, up_pre, (jax.nn.gelu(gate_pre) * up_pre).astype(BF)

    second_in, gate_pre, up_pre, hidden = step(
        feed, second_own, second_x, second_core, second_both, gate_other, up_other
    )

    totals = ReplicaTotals(line, 14)
    tile_rows = width // 2

    def tile_in(piece):
        def tile(left, right):
            near = left[:, piece * tile_rows : (piece + 1) * tile_rows]
            far = left[:, width + piece * tile_rows : width + (piece + 1) * tile_rows]
            return contract_rows(far, right).astype(BF), contract_rows(near, right).astype(BF)

        return tile

    def tile_out(piece):
        def tile(left, right):
            left = left[:, piece * tile_rows : (piece + 1) * tile_rows]
            return (
                contract_rows(left, right[:, width:]).astype(BF),
                contract_rows(left, right[:, :width]).astype(BF),
            )

        return tile

    totals.start(tile_out(0), hidden, grad_rows)
    totals.start(tile_out(1), hidden, grad_rows)
    down_other = step(join_halves, down_half, down_swap)

    def feed_back(grads, gate, up, down_o):
        grad_hidden = contract_cols(grads[:, :width], down_weight) + contract_cols(
            grads[:, width:], down_o
        )
        value, pull = jax.vjp(jax.nn.gelu, gate)
        return pull(grad_hidden * up)[0].astype(BF), (grad_hidden * value).astype(BF)

    grad_gate, grad_up = step(feed_back, grad_rows, gate_pre, up_pre, down_other)

    def back_half(rows, low, terms):
        flat = [value for term in terms for value in term]

        def total(*held):
            out = []
            for side in (1, 2):
                part = None
                for index in range(len(terms)):
                    grad, weight = held[3 * index], held[3 * index + side]
                    value = contract_cols(grad[rows], weight)
                    part = value if part is None else part + value
                out.append(part.astype(BF) if low else part)
            return jnp.concatenate(out, 1)

        return step(total, *flat)

    feed_terms = ((grad_gate, gate_weight, gate_other), (grad_up, up_weight, up_other))
    back = back_half(slice(half_rows, None), True, feed_terms)
    second_from_core = move(back, TO_CORE)
    totals.turn(0)
    totals.start(tile_in(0), second_in, grad_gate)
    front = back_half(slice(0, half_rows), False, feed_terms)
    own_second, second_away = reduce_row(front, second_from_core)
    totals.turn(1)
    totals.start(tile_in(1), second_in, grad_gate)

    def middle(own, away, normed, inverse, gain, own_grad):
        grad_in, gain_part = norm_back(own + away.astype(F32), normed, inverse, gain)
        mid = own_grad.astype(F32) + grad_in
        return mid, mid.astype(BF), gain_part

    grad_mid, attn_own, second_gain_part = step(
        middle, own_second, second_away, second_normed, second_inv, second_gain_full, grad_half[:quarter]
    )
    attn_x, attn_core = gather_start(attn_own)
    totals.turn(2)
    totals.start(tile_in(0), second_in, grad_up)
    attn_x = take(attn_x)
    attn_both = move(attn_x, TO_CORE)
    totals.turn(3)
    totals.start(tile_in(1), second_in, grad_up)

    def gated_back(own, from_x, core, both, output_o):
        rows = jnp.concatenate((own, from_x, core, both), 0)
        return rows, contract_cols(rows[:, :width], output_weight) + contract_cols(
            rows[:, width:], output_o
        )

    attn_in, grad_gated = step(gated_back, attn_own, attn_x, attn_core, attn_both, output_other)
    totals.turn(4)
    totals.start(tile_out(0), gated, attn_in)

    def head_back(grad_head, swish, gain, normed, inverse, open_floor):
        swish_out, pull = jax.vjp(jax.nn.silu, swish)
        gain_part = jnp.sum(grad_head * swish_out * normed, 0)
        product = grad_head * gain
        grad_normed = product * swish_out
        grad_swish = pull(product * normed)[0].astype(BF)
        grad_retained = (
            inverse
            * (
                grad_normed
                - jnp.mean(grad_normed, 1, keepdims=True)
                - open_floor * normed * jnp.mean(grad_normed * normed, 1, keepdims=True)
            )
        ).astype(BF)
        return gain_part, grad_swish, grad_retained

    heads = [
        step(
            head_back,
            grad_gated[:, values[head]],
            swish_in[:, values[head]],
            group_gains[head],
            *retained[head],
        )
        for head in range(2)
    ]
    group_gain_parts = [head[0] for head in heads]
    grad_swish = step(lambda a, b: jnp.concatenate((a, b), 1), heads[0][1], heads[1][1])
    totals.turn(5)
    totals.start(tile_out(1), gated, attn_in)

    def retain_back(grad, weighted, value, mask, q, w, cos, sin):
        grad_value = contract_rows(weighted, grad).astype(BF)
        grad_scores = (contract_cols(grad, value) * mask).astype(BF)
        return (
            grad_value,
            rotate_back(dot(grad_scores, w), cos, sin).astype(BF),
            rotate_back(contract_rows(grad_scores, q), cos, sin).astype(BF),
        )

    backs = []
    for head in range(2):
        backs.append(
            step(
                retain_back,
                heads[head][2],
                scores[head],
                valued[:, values[head]],
                masks[head],
                query_rot[head],
                key_rot[head],
                cosine,
                sine,
            )
        )
        totals.turn(6 + head)
        totals.start(tile_in(head), first_in, grad_swish)
    grad_value, grad_query, grad_key, grad_query_key = step(
        lambda v0, q0, k0, v1, q1, k1: (
            jnp.concatenate((v0, v1), 1),
            jnp.concatenate((q0, q1), 1),
            jnp.concatenate((k0, k1), 1),
            jnp.concatenate((q0, q1, k0, k1), 1),
        ),
        *backs[0],
        *backs[1],
    )
    head_terms = (
        (grad_query, query_weight, query_other),
        (grad_key, key_weight, key_other),
        (grad_value, value_weight, value_other),
        (grad_swish, swish_weight, swish_other),
    )
    back = back_half(slice(half_rows, None), True, head_terms)
    first_from_core = move(back, TO_CORE)
    totals.turn(8)
    totals.start(tile_in(0), first_in, grad_value)
    front = back_half(slice(0, half_rows), False, head_terms)
    own_first, first_away = reduce_row(front, first_from_core)
    totals.turn(9)
    totals.start(tile_in(1), first_in, grad_value)

    def last(own, away, rows, gain, mid):
        normed, inverse = normalize(rows)
        grad_in, gain_part = norm_back(own + away.astype(F32), normed, inverse, gain)
        return mid + grad_in, gain_part

    input_own, first_gain_part = step(
        last, own_first, first_away, own_input, first_gain_full, grad_mid
    )
    totals.turn(10)
    totals.start(tile_in(0), first_in, grad_query_key)
    input_grad = home(input_own)
    totals.turn(11)
    totals.start(tile_in(1), first_in, grad_query_key)
    own_down, down_away = project_scatter(hidden, down_weight, down_other)
    totals.turn(12)
    block_own = step(
        lambda mid, own, away: (mid + own + away.astype(F32)).astype(BF), x_mid, own_down, down_away
    )
    block_out = home(block_own)
    totals.turn(13)
    for index in range(14, 14 + LAG + 1):
        totals.turn(index)
    finals = totals.finals
    down_grad, gate_grad, up_grad, output_grad, swish_grad, value_grad, query_key_grad = (
        jnp.concatenate((finals[2 * i], finals[2 * i + 1]), 0) for i in range(7)
    )
    query_grad, key_grad = query_key_grad[:, :head_cols], query_key_grad[:, head_cols:]

    group_pair = jnp.where(
        y == 0,
        jnp.stack(group_gain_parts),
        jnp.stack(group_gain_parts[::-1]),
    )
    outgoing = jnp.concatenate((first_gain_part[width:], second_gain_part[width:], group_pair[1]))
    incoming = move(outgoing, TO_COL)
    gains = jnp.concatenate((first_gain_part[:width], second_gain_part[:width])) + incoming[: 2 * width]
    gains = gains + move(gains, TO_CORE)
    gains = gains + move(gains, TO_X)
    gains = jnp.concatenate((gains, group_pair[0] + incoming[2 * width :]))
    if lax.axis_size("dp") == 4:
        gains = gains + lax.ppermute(gains, "dp", OUTER)
        gains = gains + lax.ppermute(gains, "dp", [(0, 3), (3, 0), (1, 2), (2, 1)])
    else:
        gains = lax.psum(gains, "dp")
    group_gain_grad = gains[2 * width :]
    return (
        block_out,
        input_grad,
        gains[:width],
        query_grad,
        key_grad,
        value_grad,
        swish_grad,
        group_gain_grad,
        output_grad,
        gains[width : 2 * width],
        gate_grad,
        up_grad,
        down_grad,
    )


def solution(mesh):
    placed = (
        P(("dp", "row"), "col"),
        P(("dp", "row"), "col"),
        P("col"),
        P("col", "row"),
        P("col", "row"),
        P("col", "row"),
        P("col", "row"),
        P(("row", "col")),
        P("row", "col"),
        P("col"),
        P("col", "row"),
        P("col", "row"),
        P("row", "col"),
        P(("row", "col")),
    )
    return jax.shard_map(
        body,
        mesh=mesh,
        in_specs=placed,
        out_specs=(
            P(("dp", "row"), "col"),
            P(("dp", "row"), "col"),
            P("col"),
            P("col", "row"),
            P("col", "row"),
            P("col", "row"),
            P("col", "row"),
            P(("row", "col")),
            P("row", "col"),
            P("col"),
            P("col", "row"),
            P("col", "row"),
            P("row", "col"),
        ),
        check_vma=False,
    )
```

```python
import jax
import jax.numpy as jnp
from jax import lax
from jax.experimental import pallas as pl
from jax.experimental.pallas import tpu as pltpu
from jax.sharding import PartitionSpec as P

LEN = 1024
EPS = 1e-05
ROTARY_BASE = 10000.0
BF = jnp.bfloat16
F32 = jnp.float32
RC = ("row", "col")


def grid_perm(target):
    pairs = []
    for row in range(4):
        for col in range(2):
            place = target(row // 2, row % 2, col)
            if place is not None:
                pairs.append((row * 2 + col, (place[0] * 2 + place[1]) * 2 + place[2]))
    return pairs


TO_COL = grid_perm(lambda x, k, y: (x, k, 1 - y))
TO_X = grid_perm(lambda x, k, y: (1 - x, k, y))
TO_CORE = grid_perm(lambda x, k, y: (x, 1 - k, y))
SEQ_IN = grid_perm(lambda x, k, y: (1 - x, k, y) if x == y else (x, k, 1 - y))
SEQ_OUT = grid_perm(lambda x, k, y: (x, k, 1 - y) if x == y else (1 - x, k, y))
CROSS = grid_perm(lambda x, k, y: (1 - x, k, 1 - y) if x != y else None)


class Line:
    def __init__(self):
        self.token = lax.create_token()

    def take(self, *values):
        *held, self.token = lax.optimization_barrier(values + (self.token,))
        return held[0] if len(held) == 1 else tuple(held)

    def step(self, work, *inputs):
        held = self.take(*inputs)
        results = work(*held) if len(inputs) > 1 else work(held)
        return self.take(*results) if isinstance(results, tuple) else self.take(results)


def move(value, pairs):
    return lax.ppermute(value, RC, pairs)


def dot(left, right):
    return jnp.dot(left, right, preferred_element_type=F32)


def contract_rows(left, right):
    return lax.dot_general(left, right, (((0,), (0,)), ((), ())), preferred_element_type=F32)


def contract_cols(left, right):
    return lax.dot_general(left, right, (((1,), (1,)), ((), ())), preferred_element_type=F32)


def normalize(rows):
    average = jnp.mean(rows, 1, keepdims=True)
    centred = rows - average
    variance = jnp.mean(centred * centred, 1, keepdims=True)
    inverse = lax.rsqrt(variance + EPS)
    return centred * inverse, inverse


def norm_back(grad_rows, normed, inverse, gain):
    scaled = grad_rows * gain
    grad_in = inverse * (
        scaled
        - jnp.mean(scaled, 1, keepdims=True)
        - normed * jnp.mean(scaled * normed, 1, keepdims=True)
    )
    return grad_in, jnp.sum(grad_rows * normed, 0)


def rotate(values, cosine, sine):
    half = values.shape[1] // 2
    front, back = values[:, :half], values[:, half:]
    return jnp.concatenate((front * cosine - back * sine, front * sine + back * cosine), 1)


def rotate_back(values, cosine, sine):
    half = values.shape[1] // 2
    front, back = values[:, :half], values[:, half:]
    return jnp.concatenate((front * cosine + back * sine, back * cosine - front * sine), 1)


VMEM_BYTES = 56 * 1024 * 1024
BLOCK = 256


def call(body, grid, ins, in_specs, outs, out_specs, scratch=()):
    return pl.pallas_call(
        body,
        grid=grid,
        in_specs=in_specs,
        out_specs=out_specs,
        out_shape=outs,
        scratch_shapes=list(scratch),
        compiler_params=pltpu.CompilerParams(
            vmem_limit_bytes=VMEM_BYTES, dimension_semantics=("arbitrary",) * len(grid)
        ),
    )(*ins)


SCALARS = pl.BlockSpec(memory_space=pltpu.SMEM)


def decay_block(scalars, rates, head, i, j):
    base = scalars[0]
    apart = ((base ^ i) - (base ^ j)) * BLOCK
    distance = (
        apart
        + lax.broadcasted_iota(jnp.int32, (BLOCK, BLOCK), 0)
        - lax.broadcasted_iota(jnp.int32, (BLOCK, BLOCK), 1)
    )
    lag = jnp.maximum(distance, 0).astype(F32)
    return jnp.where(distance >= 0, jnp.exp(-rates[head] * lag), 0.0)


def retention(scalars, rates, query, key, value):
    tokens = query.shape[0]
    size, out_size = query.shape[1] // 2, value.shape[1] // 2
    blocks = tokens // BLOCK

    def body(scalar_ref, rate_ref, q_ref, k_ref, v_ref, normed_ref, inverse_ref, open_ref, sums):
        head = pl.program_id(0)
        base = scalar_ref[0]
        for i in range(blocks):
            rows = pl.ds(i * BLOCK, BLOCK)
            sums[...] = jnp.zeros(sums.shape, F32)
            q = q_ref[rows, :]
            for j in range(blocks):
                @pl.when((base ^ i) >= (base ^ j))
                def _():
                    columns = pl.ds(j * BLOCK, BLOCK)
                    mask = decay_block(scalar_ref, rate_ref, head, i, j)
                    weighted = (contract_cols(q, k_ref[columns, :]) * mask).astype(BF)
                    sums[...] += dot(weighted, v_ref[columns, :])

            total = sums[...]
            average = jnp.mean(total, 1, keepdims=True)
            centred = total - average
            variance = jnp.mean(centred * centred, 1, keepdims=True)
            inverse = lax.rsqrt(jnp.maximum(variance, 1.0))
            normed_ref[rows, :] = centred * inverse
            inverse_ref[0, rows, :] = inverse
            open_ref[0, rows, :] = jnp.where(variance > 1.0, 1.0, 0.0)

    head_block = lambda columns: pl.BlockSpec((tokens, columns), lambda h: (0, h))
    column = pl.BlockSpec((1, tokens, 1), lambda h: (h, 0, 0))
    return call(
        body,
        (2,),
        [scalars, rates, query, key, value],
        [SCALARS, SCALARS, head_block(size), head_block(size), head_block(out_size)],
        [
            jax.ShapeDtypeStruct((tokens, 2 * out_size), F32),
            jax.ShapeDtypeStruct((2, tokens, 1), F32),
            jax.ShapeDtypeStruct((2, tokens, 1), F32),
        ],
        [head_block(out_size), column, column],
        [pltpu.VMEM((BLOCK, out_size), F32)],
    )


def retention_back(scalars, rates, query, key, value, grad, cosine, sine):
    tokens = query.shape[0]
    size, out_size = query.shape[1] // 2, value.shape[1] // 2
    blocks = tokens // BLOCK

    def body(
        scalar_ref, rate_ref, q_ref, k_ref, v_ref, g_ref, cos_ref, sin_ref,
        gv_ref, gq_ref, gk_ref, q_sum, k_sum, v_sum,
    ):
        head = pl.program_id(0)
        base = scalar_ref[0]
        k_sum[...] = jnp.zeros(k_sum.shape, F32)
        v_sum[...] = jnp.zeros(v_sum.shape, F32)
        for i in range(blocks):
            rows = pl.ds(i * BLOCK, BLOCK)
            q_sum[...] = jnp.zeros(q_sum.shape, F32)
            q, g = q_ref[rows, :], g_ref[rows, :]
            for j in range(blocks):
                @pl.when((base ^ i) >= (base ^ j))
                def _():
                    columns = pl.ds(j * BLOCK, BLOCK)
                    mask = decay_block(scalar_ref, rate_ref, head, i, j)
                    k = k_ref[columns, :]
                    weighted = (contract_cols(q, k) * mask).astype(BF)
                    v_sum[columns, :] += contract_rows(weighted, g)
                    scores = (contract_cols(g, v_ref[columns, :]) * mask).astype(BF)
                    q_sum[...] += dot(scores, k)
                    k_sum[columns, :] += contract_rows(scores, q)

            gq_ref[rows, :] = rotate_back(q_sum[...], cos_ref[rows, :], sin_ref[rows, :]).astype(BF)
        for j in range(blocks):
            columns = pl.ds(j * BLOCK, BLOCK)
            gk_ref[columns, :] = rotate_back(
                k_sum[columns, :], cos_ref[columns, :], sin_ref[columns, :]
            ).astype(BF)
            gv_ref[columns, :] = v_sum[columns, :].astype(BF)

    head_block = lambda columns: pl.BlockSpec((tokens, columns), lambda h: (0, h))
    table = pl.BlockSpec(cosine.shape, lambda h: (0, 0))
    return call(
        body,
        (2,),
        [scalars, rates, query, key, value, grad, cosine, sine],
        [SCALARS, SCALARS, head_block(size), head_block(size)]
        + [head_block(out_size)] * 2
        + [table, table],
        [
            jax.ShapeDtypeStruct((tokens, 2 * out_size), BF),
            jax.ShapeDtypeStruct((tokens, 2 * size), BF),
            jax.ShapeDtypeStruct((tokens, 2 * size), BF),
        ],
        [head_block(out_size), head_block(size), head_block(size)],
        [
            pltpu.VMEM((BLOCK, size), F32),
            pltpu.VMEM((tokens, size), F32),
            pltpu.VMEM((tokens, out_size), F32),
        ],
    )


OUTER = [(0, 1), (1, 0), (2, 3), (3, 2)]
INNER = [(1, 2), (2, 1)]
LAG = 3


class ReplicaTotals:
    def __init__(self, line, count):
        self.line = line
        self.count = count
        self.four = lax.axis_size("dp") == 4
        place = lax.axis_index("dp")
        self.outer = (place == 0) | (place == 3)
        self.mine, self.far, self.parts, self.got = [], [], [], []
        self.local, self.other, self.totals, self.finals = [], [], [], []

    def start(self, tile, *inputs):
        far, mine = self.line.step(lambda *held: tile(*held), *inputs)
        self.far.append(move(far, TO_COL))
        self.mine.append(mine)

    def turn(self, index):
        if not self.four:
            if index < self.count:
                part = self.line.step(
                    lambda mine, far: (mine.astype(F32) + far.astype(F32)).astype(BF),
                    self.mine[index],
                    self.far[index],
                )
                self.finals.append(lax.psum(part, "dp").astype(F32))
            return
        count = self.count
        back = index - LAG
        if index < count:
            if back >= 0:
                def join(mine, far, total):
                    part = (mine.astype(F32) + far.astype(F32)).astype(BF)
                    return part, jnp.where(self.outer, part, total)

                part, sent = self.line.step(
                    join, self.mine[index], self.far[index], self.totals[back]
                )
            else:
                part = self.line.step(
                    lambda mine, far: (mine.astype(F32) + far.astype(F32)).astype(BF),
                    self.mine[index],
                    self.far[index],
                )
                sent = part
            self.parts.append(part)
            self.got.append(lax.ppermute(sent, "dp", OUTER))
        elif index < count + LAG:
            self.got.append(lax.ppermute(self.totals[back], "dp", OUTER))

        before = index - 1
        if 0 <= before < count:
            local = self.line.step(
                lambda part, got: (part.astype(F32) + got.astype(F32)).astype(BF),
                self.parts[before],
                self.got[before],
            )
            self.local.append(local)
            self.other.append(lax.ppermute(local, "dp", INNER))
        earlier = index - 2
        if 0 <= earlier < count:
            self.totals.append(
                self.line.step(
                    lambda local, other: (local.astype(F32) + other.astype(F32)).astype(BF),
                    self.local[earlier],
                    self.other[earlier],
                )
            )
        ready = before - LAG
        if 0 <= ready < count:
            self.finals.append(
                self.line.step(
                    lambda got, total: jnp.where(self.outer, got, total).astype(F32),
                    self.got[before],
                    self.totals[ready],
                )
            )


def body(
    tokens,
    grad_out,
    first_gain,
    query_weight,
    key_weight,
    value_weight,
    swish_weight,
    group_gain,
    output_weight,
    second_gain,
    gate_weight,
    up_weight,
    down_weight,
    decay_rate,
):
    row = lax.axis_index("row")
    y = lax.axis_index("col")
    place = lax.axis_index("dp")
    x, k = row // 2, row % 2
    parity = place % 2
    same = x == y
    rows_dev, width = tokens.shape
    quarter = rows_dev // 2

    def sequence_rows(block, got, cross):
        mine = jnp.where(same, block, got)
        other = jnp.where(same, got, cross)
        both = jnp.concatenate((mine, other), 1)
        return jnp.concatenate(
            (
                lax.dynamic_slice_in_dim(both, x * quarter, quarter, 0),
                lax.dynamic_slice_in_dim(both, (1 - x) * quarter, quarter, 0),
            ),
            0,
        )

    def home(rows):
        mine, other = rows[:, :width], rows[:, width:]
        got = move(jnp.where(same, other, mine).astype(BF), SEQ_OUT)
        cross = move(other.astype(BF), CROSS)
        here = jnp.where(same, mine, got.astype(rows.dtype))
        there = jnp.where(same, got, cross).astype(rows.dtype)
        return jnp.where(
            x == 0, jnp.concatenate((here, there), 0), jnp.concatenate((there, here), 0)
        )

    head_values = group_gain.shape[0]
    small = jnp.concatenate((first_gain, second_gain, group_gain, decay_rate))
    small_other = move(small, TO_COL)
    line = Line()
    scalars = jnp.stack([2 * k + x, parity, x, k]).astype(jnp.int32)
    step, take = line.step, line.take

    count = lax.axis_size("dp")
    even = parity == 0
    swap = [(i, i ^ 1) for i in range(count)]

    def send_half(block):
        half = block.shape[0] // 2
        return lax.dynamic_slice_in_dim(block, parity * half, half, 0)

    def join_halves(first, second):
        return jnp.concatenate(
            (jnp.where(even, first, second), jnp.where(even, second, first)), 0
        )

    def over_dp(value):
        return lax.ppermute(value, "dp", swap)

    def over_col(value):
        return move(value, TO_COL)

    base = 2 * k + x
    block_ids = jnp.bitwise_xor(base, jnp.arange(4, dtype=jnp.int32))
    positions = (
        block_ids[:, None] * quarter + jnp.arange(quarter, dtype=jnp.int32)[None, :]
    ).reshape(-1)
    key_size = query_weight.shape[1] // 2
    value_size = value_weight.shape[1] // 2
    half_key = key_size // 2
    frequency = ROTARY_BASE ** (-jnp.arange(half_key, dtype=F32) / half_key)
    rotation = positions.astype(F32)[:, None] * frequency[None, :]
    distance = positions[:, None] - positions[None, :]
    lag = jnp.maximum(distance, 0).astype(F32)
    head_cols = query_weight.shape[1]
    values = [slice(head * value_size, (head + 1) * value_size) for head in range(2)]

    token_seq, token_cross = move(tokens, SEQ_IN), move(tokens, CROSS)
    query_key_half = over_col(
        step(lambda q, w: send_half(jnp.concatenate((q, w), 1)), query_weight, key_weight)
    )
    cosine, sine = step(lambda turns: (jnp.cos(turns), jnp.sin(turns)), rotation)

    def first_norm(block, got, cross, other_small):
        gain = jnp.concatenate((first_gain, other_small[:width]))
        rows = sequence_rows(block, got, cross).astype(F32)
        normed, inverse = normalize(rows)
        return (normed * gain).astype(BF), rows[:quarter]

    value_half = over_col(step(send_half, value_weight))
    first_half, own_input = step(first_norm, tokens, token_seq, token_cross, small_other)
    first_core = move(first_half, TO_CORE)
    swish_half = over_col(step(send_half, swish_weight))
    second_gain_full = jnp.concatenate((second_gain, small_other[width : 2 * width]))
    first_gain_full = jnp.concatenate((first_gain, small_other[:width]))
    own_group = (group_gain, small_other[2 * width : 2 * width + head_values])
    own_rate = (decay_rate[0], small_other[2 * width + head_values])
    group_gains = tuple(jnp.where(y == 0, own_group[i], own_group[1 - i]) for i in range(2))
    rates = jnp.stack([jnp.where(y == 0, own_rate[i], own_rate[1 - i]) for i in range(2)])

    query_key_half = take(query_key_half)
    query_key_swap = over_dp(query_key_half)

    def mine_first(half, core):
        full = jnp.concatenate((half, core), 0)
        rows = full[:, :width]
        return (
            full,
            dot(rows, query_weight),
            dot(rows, key_weight),
            dot(rows, value_weight),
            dot(rows, swish_weight),
        )

    first_in, query_mine, key_mine, value_mine, swish_mine = step(mine_first, first_half, first_core)
    output_send = step(send_half, output_weight)
    value_half = take(value_half)
    value_swap = over_dp(value_half)
    output_half = over_col(output_send)

    def other_query_key(rows, half, swapped, query, key, cos, sin):
        other = join_halves(half, swapped)
        rows = rows[:, width:]
        query = query + dot(rows, other[:, :head_cols])
        key = key + dot(rows, other[:, head_cols:])
        out = [other]
        for total in (query, key):
            out.append(
                jnp.concatenate(
                    [
                        rotate(total[:, h * key_size : (h + 1) * key_size], cos, sin)
                        for h in range(2)
                    ],
                    1,
                ).astype(BF)
            )
        return tuple(out)

    query_key_other, query_rot, key_rot = step(
        other_query_key, first_in, query_key_half, query_key_swap, query_mine, key_mine, cosine, sine
    )
    query_other, key_other = query_key_other[:, :head_cols], query_key_other[:, head_cols:]

    swish_half = take(swish_half)
    swish_swap = over_dp(swish_half)

    def other_value(rows, half, swapped, value):
        other = join_halves(half, swapped)
        return other, (value + dot(rows[:, width:], other)).astype(BF)

    value_other, valued = step(other_value, first_in, value_half, value_swap, value_mine)
    grad_held = take(grad_out)
    grad_seq, grad_cross = move(grad_held, SEQ_IN), move(grad_held, CROSS)

    normed, group_inv, group_open = step(
        lambda *held: tuple(retention(scalars, rates, *held)), query_rot, key_rot, valued
    )
    output_half = take(output_half)
    output_swap = over_dp(output_half)
    gate_half = over_col(step(send_half, gate_weight))

    wide_gain = jnp.concatenate(group_gains)

    def gating(rows, half, swapped, mine, normed, gains):
        other = join_halves(half, swapped)
        swish = mine + dot(rows[:, width:], other)
        return other, swish, (jax.nn.silu(swish) * normed * gains).astype(BF)

    swish_other, swish_in, gated = step(
        gating, first_in, swish_half, swish_swap, swish_mine, normed, wide_gain
    )
    up_half = over_col(step(send_half, up_weight))
    grad_half = step(sequence_rows, grad_out, grad_seq, grad_cross)
    grad_core = move(grad_half, TO_CORE)

    half_rows = 2 * quarter

    def project(rows, mine, other):
        return dot(rows, mine), dot(rows, other)

    def project_scatter(rows, mine, other):
        back = step(
            lambda r, m, o: jnp.concatenate(
                (dot(r, m).astype(BF), dot(r, o).astype(BF)), 1
            ),
            rows[half_rows:],
            mine,
            other,
        )
        from_core = move(back, TO_CORE)
        front = step(
            lambda r, m, o: jnp.concatenate((dot(r, m), dot(r, o)), 1), rows[:half_rows], mine, other
        )
        return reduce_row(front, from_core)

    def reduce_row(front, from_core):
        def add(part, core):
            both = part + core.astype(F32)
            return both[:quarter], both[quarter:].astype(BF)

        own, away = step(add, front, from_core)
        return own, move(away, TO_X)

    output_other = step(join_halves, output_half, output_swap)
    gate_half = take(gate_half)
    gate_swap = over_dp(gate_half)
    own_out, out_x = project_scatter(gated, output_weight, output_other)
    grad_rows = step(lambda a, b: jnp.concatenate((a, b), 0), grad_half, grad_core)
    down_half = over_col(step(send_half, down_weight))

    def second_norm(rows, own, away, gain):
        mid = rows + own + away.astype(F32)
        normed, inverse = normalize(mid)
        return mid, normed, inverse, (normed * gain).astype(BF)

    x_mid, second_normed, second_inv, second_own = step(
        second_norm, own_input, own_out, out_x, second_gain_full
    )

    def gather_start(own):
        return move(own, TO_X), move(own, TO_CORE)

    second_x, second_core = gather_start(second_own)
    up_half = take(up_half)
    up_swap = over_dp(up_half)
    gate_other = step(join_halves, gate_half, gate_swap)
    second_x = take(second_x)
    second_both = move(second_x, TO_CORE)
    up_other = step(join_halves, up_half, up_swap)
    down_half = take(down_half)
    down_swap = over_dp(down_half)

    def feed(own, from_x, core, both, gate_o, up_o):
        rows = jnp.concatenate((own, from_x, core, both), 0)
        near, far = rows[:, :width], rows[:, width:]
        gate_pre = dot(near, gate_weight) + dot(far, gate_o)
        up_pre = dot(near, up_weight) + dot(far, up_o)
        return rows, gate_pre, up_pre, (jax.nn.gelu(gate_pre) * up_pre).astype(BF)

    second_in, gate_pre, up_pre, hidden = step(
        feed, second_own, second_x, second_core, second_both, gate_other, up_other
    )

    totals = ReplicaTotals(line, 14)
    tile_rows = width // 2

    def tile_in(piece):
        def tile(left, right):
            near = left[:, piece * tile_rows : (piece + 1) * tile_rows]
            far = left[:, width + piece * tile_rows : width + (piece + 1) * tile_rows]
            return contract_rows(far, right).astype(BF), contract_rows(near, right).astype(BF)

        return tile

    def tile_out(piece):
        def tile(left, right):
            left = left[:, piece * tile_rows : (piece + 1) * tile_rows]
            return (
                contract_rows(left, right[:, width:]).astype(BF),
                contract_rows(left, right[:, :width]).astype(BF),
            )

        return tile

    totals.start(tile_out(0), hidden, grad_rows)
    down_other = step(join_halves, down_half, down_swap)

    def feed_back(grads, gate, up, down_o):
        grad_hidden = contract_cols(grads[:, :width], down_weight) + contract_cols(
            grads[:, width:], down_o
        )
        value, pull = jax.vjp(jax.nn.gelu, gate)
        return pull(grad_hidden * up)[0].astype(BF), (grad_hidden * value).astype(BF)

    grad_gate, grad_up = step(feed_back, grad_rows, gate_pre, up_pre, down_other)
    totals.start(tile_out(1), hidden, grad_rows)

    def back_half(rows, low, terms):
        flat = [value for term in terms for value in term]

        def total(*held):
            out = []
            for side in (1, 2):
                part = None
                for index in range(len(terms)):
                    grad, weight = held[3 * index], held[3 * index + side]
                    value = contract_cols(grad[rows], weight)
                    part = value if part is None else part + value
                out.append(part.astype(BF) if low else part)
            return jnp.concatenate(out, 1)

        return step(total, *flat)

    feed_terms = ((grad_gate, gate_weight, gate_other), (grad_up, up_weight, up_other))
    back = back_half(slice(half_rows, None), True, feed_terms)
    second_from_core = move(back, TO_CORE)
    totals.turn(0)
    totals.start(tile_in(0), second_in, grad_gate)
    front = back_half(slice(0, half_rows), False, feed_terms)
    own_second, second_away = reduce_row(front, second_from_core)
    totals.turn(1)
    totals.start(tile_in(1), second_in, grad_gate)

    def middle(own, away, normed, inverse, gain, own_grad):
        grad_in, gain_part = norm_back(own + away.astype(F32), normed, inverse, gain)
        mid = own_grad.astype(F32) + grad_in
        return mid, mid.astype(BF), gain_part

    grad_mid, attn_own, second_gain_part = step(
        middle, own_second, second_away, second_normed, second_inv, second_gain_full, grad_half[:quarter]
    )
    attn_x, attn_core = gather_start(attn_own)
    totals.turn(2)
    totals.start(tile_in(0), second_in, grad_up)
    attn_x = take(attn_x)
    attn_both = move(attn_x, TO_CORE)
    totals.turn(3)
    totals.start(tile_in(1), second_in, grad_up)

    def gated_back(own, from_x, core, both, output_o):
        rows = jnp.concatenate((own, from_x, core, both), 0)
        return rows, contract_cols(rows[:, :width], output_weight) + contract_cols(
            rows[:, width:], output_o
        )

    attn_in, grad_gated = step(gated_back, attn_own, attn_x, attn_core, attn_both, output_other)
    totals.turn(4)
    totals.start(tile_out(0), gated, attn_in)

    def head_back(grad_head, swish, gain, normed, inverse, open_floor):
        swish_out, pull = jax.vjp(jax.nn.silu, swish)
        gain_part = jnp.sum(grad_head * swish_out * normed, 0)
        product = grad_head * gain
        grad_normed = product * swish_out
        grad_swish = pull(product * normed)[0].astype(BF)
        grad_retained = (
            inverse
            * (
                grad_normed
                - jnp.mean(grad_normed, 1, keepdims=True)
                - open_floor * normed * jnp.mean(grad_normed * normed, 1, keepdims=True)
            )
        ).astype(BF)
        return gain_part, grad_swish, grad_retained

    heads = [
        step(
            head_back,
            grad_gated[:, values[head]],
            swish_in[:, values[head]],
            group_gains[head],
            normed[:, values[head]],
            group_inv[head],
            group_open[head],
        )
        for head in range(2)
    ]
    group_gain_parts = [head[0] for head in heads]
    grad_swish = step(lambda a, b: jnp.concatenate((a, b), 1), heads[0][1], heads[1][1])
    totals.turn(5)
    totals.start(tile_out(1), gated, attn_in)

    grad_retained = step(lambda a, b: jnp.concatenate((a, b), 1), heads[0][2], heads[1][2])
    totals.turn(6)
    totals.start(tile_in(0), first_in, grad_swish)
    grad_value, grad_query, grad_key = step(
        lambda *held: tuple(retention_back(scalars, rates, *held)),
        query_rot, key_rot, valued, grad_retained, cosine, sine,
    )
    totals.turn(7)
    totals.start(tile_in(1), first_in, grad_swish)
    grad_query_key = step(lambda a, b: jnp.concatenate((a, b), 1), grad_query, grad_key)
    head_terms = (
        (grad_query, query_weight, query_other),
        (grad_key, key_weight, key_other),
        (grad_value, value_weight, value_other),
        (grad_swish, swish_weight, swish_other),
    )
    back = back_half(slice(half_rows, None), True, head_terms)
    first_from_core = move(back, TO_CORE)
    totals.turn(8)
    totals.start(tile_in(0), first_in, grad_value)
    front = back_half(slice(0, half_rows), False, head_terms)
    own_first, first_away = reduce_row(front, first_from_core)
    totals.turn(9)
    totals.start(tile_in(1), first_in, grad_value)

    def last(own, away, rows, gain, mid):
        normed, inverse = normalize(rows)
        grad_in, gain_part = norm_back(own + away.astype(F32), normed, inverse, gain)
        return mid + grad_in, gain_part

    input_own, first_gain_part = step(
        last, own_first, first_away, own_input, first_gain_full, grad_mid
    )
    totals.turn(10)
    totals.start(tile_in(0), first_in, grad_query_key)
    input_grad = home(input_own)
    totals.turn(11)
    totals.start(tile_in(1), first_in, grad_query_key)
    own_down, down_away = project_scatter(hidden, down_weight, down_other)
    totals.turn(12)
    block_own = step(
        lambda mid, own, away: (mid + own + away.astype(F32)).astype(BF), x_mid, own_down, down_away
    )
    block_out = home(block_own)
    totals.turn(13)
    for index in range(14, 14 + LAG + 1):
        totals.turn(index)
    finals = totals.finals
    down_grad, gate_grad, up_grad, output_grad, swish_grad, value_grad, query_key_grad = (
        jnp.concatenate((finals[2 * i], finals[2 * i + 1]), 0) for i in range(7)
    )
    query_grad, key_grad = query_key_grad[:, :head_cols], query_key_grad[:, head_cols:]

    group_pair = jnp.where(
        y == 0,
        jnp.stack(group_gain_parts),
        jnp.stack(group_gain_parts[::-1]),
    )
    outgoing = jnp.concatenate((first_gain_part[width:], second_gain_part[width:], group_pair[1]))
    incoming = move(outgoing, TO_COL)
    gains = jnp.concatenate((first_gain_part[:width], second_gain_part[:width])) + incoming[: 2 * width]
    gains = gains + move(gains, TO_CORE)
    gains = gains + move(gains, TO_X)
    gains = jnp.concatenate((gains, group_pair[0] + incoming[2 * width :]))
    if lax.axis_size("dp") == 4:
        gains = gains + lax.ppermute(gains, "dp", OUTER)
        gains = gains + lax.ppermute(gains, "dp", [(0, 3), (3, 0), (1, 2), (2, 1)])
    else:
        gains = lax.psum(gains, "dp")
    group_gain_grad = gains[2 * width :]
    return (
        block_out,
        input_grad,
        gains[:width],
        query_grad,
        key_grad,
        value_grad,
        swish_grad,
        group_gain_grad,
        output_grad,
        gains[width : 2 * width],
        gate_grad,
        up_grad,
        down_grad,
    )


def solution(mesh):
    placed = (
        P(("dp", "row"), "col"),
        P(("dp", "row"), "col"),
        P("col"),
        P("col", "row"),
        P("col", "row"),
        P("col", "row"),
        P("col", "row"),
        P(("row", "col")),
        P("row", "col"),
        P("col"),
        P("col", "row"),
        P("col", "row"),
        P("row", "col"),
        P(("row", "col")),
    )
    return jax.shard_map(
        body,
        mesh=mesh,
        in_specs=placed,
        out_specs=(
            P(("dp", "row"), "col"),
            P(("dp", "row"), "col"),
            P("col"),
            P("col", "row"),
            P("col", "row"),
            P("col", "row"),
            P("col", "row"),
            P(("row", "col")),
            P("row", "col"),
            P("col"),
            P("col", "row"),
            P("col", "row"),
            P("row", "col"),
        ),
        check_vma=False,
    )
```
